32 devices in a mesh: seq: 16 (over z, y, x), heads: 2 (over core).
Axes of the slice: x: 2, y: 2, z: 4, core: 2. Of those that a mesh axis runs over, the one named last changes fastest.
Arguments:
- queries: bfloat16 [2048, 24576], P('seq', 'heads'), may hold values from -8 to 8
- latent: bfloat16 [2048, 576], P(('seq', 'heads')), may hold values from -8 to 8
- w_uk: bfloat16 [128, 128, 512], P('heads'), may hold values from -0.5 to 0.5
- w_uv: bfloat16 [128, 512, 128], P('heads'), may hold values from -0.75 to 0.75
- doc_lengths: int32 [8], replicated, may hold values from 1 to 1024, as said below
Outputs:
- attention_out: bfloat16 [2048, 16384], P('seq', 'heads')
The draws below stay inside these ranges and needn't reach their ends.
Inputs may be any that keep to these rules, and one draw needn't show every extreme that they name: `doc_lengths`: the 8 lengths sum to 2048; the next to last document has exactly 1024 tokens and the last one at most 32.
All inputs are finite; a program needn't handle non-finite values.
Results may differ from the reference program's by a relative error of at most 0.0085.
Values may be sent and summed in bfloat16 or wider, within the bound.
No kernel may reach another device: no remote copies, remote signals or barrier semaphores. Data moves between devices by JAX's collectives and lax.ppermute only.
A program may use at most 320 MiB of HBM per device.

```python
import jax
import jax.numpy as jnp
from jax import lax

H = 128
NOPE = 128
ROPE = 64
KV_RANK = 512
VDIM = 128
TOK_DEV = 128
SPAN = 8
TOKENS = 2048
DOCS = 8
DOC_MOST = 1024
LATENT = 576
N_SEQ = 16


def draw_queries(key, part):
    query_width = NOPE + ROPE
    draw_key = jax.random.fold_in(key, 11)
    drawn = jnp.clip(jax.random.normal(draw_key, (TOKENS, H, query_width), jnp.float32), -6.0, 6.0)
    return drawn.reshape(TOKENS, H * query_width).astype(jnp.bfloat16)


def draw_latent(key, part):
    draw_key = jax.random.fold_in(key, 13)
    drawn = jnp.clip(jax.random.normal(draw_key, (TOKENS, KV_RANK + ROPE), jnp.float32), -6.0, 6.0)
    return drawn.astype(jnp.bfloat16)


def draw_doc_lengths(key, part):
    length_key = jax.random.fold_in(key, 4409)
    tail_key, spread_key = jax.random.split(length_key, 2)
    count = DOCS - 2
    tail = jax.random.randint(tail_key, (), 1, TOK_DEV // 4 + 1).astype(jnp.int32)
    rest = (TOKENS - DOC_MOST - tail).astype(jnp.int32)
    base = rest // count
    extra = rest - base * count
    places = jnp.arange(count, dtype=jnp.int32)
    even = base + (places < extra).astype(jnp.int32)
    moved = jax.random.randint(spread_key, (count,), 0, base // 2 + 1).astype(jnp.int32)
    spread = even + moved - jnp.roll(moved, 1)
    return jnp.concatenate([spread, jnp.full((1,), DOC_MOST, jnp.int32), tail[None]]).astype(jnp.int32)


def block_scale(key, dims, shards, smallest, top_value):
    level, own = 1.0, jax.random.fold_in(key, 6)
    for position, parts in shards:
        draws = jnp.exp(jax.random.uniform(jax.random.fold_in(own, position), (parts,), jnp.float32, smallest / len(shards), top_value / len(shards)))
        level = level * jnp.repeat(draws, dims[position] // parts).reshape([-1 if axis == position else 1 for axis in range(len(dims))])
    return level


def gaussian(key, extent, scale, bound, shards=(), held_as=jnp.bfloat16):
    loudness = block_scale(key, extent, shards, -0.22, 0.18) if shards else 1.0
    values = jax.random.normal(key, extent, jnp.float32) * scale * loudness
    return jnp.minimum(jnp.maximum(values, -bound), bound).astype(held_as)


def setup_inputs(seed: int = 0) -> dict:
    keys = jax.random.split(jax.random.key(seed), 6)
    return {
        "queries": draw_queries(jax.random.fold_in(keys[5], 71), 0),
        "latent": draw_latent(jax.random.fold_in(keys[5], 71), 0),
        "w_uk": gaussian(keys[2], (H, NOPE, KV_RANK), NOPE ** -0.5, 0.5, ((0, 2),)),
        "w_uv": gaussian(keys[3], (H, KV_RANK, VDIM), (KV_RANK // 8) ** -0.5, 0.75, ((0, 2),)),
        "doc_lengths": draw_doc_lengths(jax.random.fold_in(keys[5], 71), 0),
    }


far_negative = -1.0e30


def document_of(doc_ends, positions):
    return jnp.sum((doc_ends[None, :] <= positions[:, None]).astype(jnp.int32), axis=1)


def reference(queries, latent, w_uk, w_uv, doc_lengths):
    query_width = NOPE + ROPE
    score_scale = query_width ** -0.5
    reach_rows = (SPAN + 1) * TOK_DEV
    doc_ends = jnp.cumsum(doc_lengths).astype(jnp.int32)
    padded = jnp.concatenate([jnp.zeros((SPAN * TOK_DEV, LATENT), latent.dtype), latent], axis=0)
    blocked = queries.reshape(N_SEQ, TOK_DEV, H, query_width)
    key_proj = w_uk.astype(jnp.float32)
    value_proj = w_uv.astype(jnp.float32)
    highest = lax.Precision.HIGHEST

    def one_block(pieces):
        query_block, block_index = pieces
        first_pos = block_index * TOK_DEV
        absorbed = jnp.einsum("thd,hdl->thl", query_block[:, :, :NOPE].astype(jnp.float32), key_proj, precision=highest).astype(jnp.bfloat16)
        joined = jnp.concatenate([absorbed, query_block[:, :, NOPE:]], axis=2)
        window = lax.dynamic_slice_in_dim(padded, first_pos, reach_rows, 0)
        raw_scores = jnp.einsum("thl,kl->thk", joined.astype(jnp.float32), window.astype(jnp.float32), precision=highest)
        query_pos = first_pos + jnp.arange(TOK_DEV, dtype=jnp.int32)
        key_pos = first_pos - SPAN * TOK_DEV + jnp.arange(reach_rows, dtype=jnp.int32)
        query_doc = document_of(doc_ends, query_pos)
        key_doc = document_of(doc_ends, key_pos)
        allowed = (key_doc[None, :] == query_doc[:, None]) & (key_pos[None, :] <= query_pos[:, None]) & (key_pos[None, :] >= 0)
        scores = jnp.where(allowed[:, None, :], raw_scores * score_scale, far_negative)
        row_top = jnp.max(scores, axis=2, keepdims=True)
        exponent = jnp.exp(scores - row_top)
        row_total = jnp.sum(exponent, axis=2)
        weights = exponent.astype(jnp.bfloat16)
        mixed_sum = jnp.einsum("thk,kl->thl", weights.astype(jnp.float32), window[:, :KV_RANK].astype(jnp.float32), precision=highest)
        attended = (mixed_sum / row_total[:, :, None]).astype(jnp.bfloat16)
        projected = jnp.einsum("thl,hlv->thv", attended.astype(jnp.float32), value_proj, precision=highest)
        return projected.astype(jnp.bfloat16).reshape(TOK_DEV, H * VDIM)

    result = lax.map(one_block, (blocked, jnp.arange(N_SEQ, dtype=jnp.int32)))
    return result.reshape(N_SEQ * TOK_DEV, H * VDIM)
```

```python
import functools
import math

import jax
import jax.numpy as jnp
from jax import lax
from jax.experimental import pallas as pl
from jax.experimental.pallas import tpu as pltpu
from jax.sharding import PartitionSpec as P

DOC_MOST = 1024
TAIL_MOST = 32
SUBS = 4
KEY_TILE = 256
LANES = 128
HEADS_STEP = 8

far_negative = -1e30


def order_bit(phase, core, bits):
    return 1 << ((phase + core) % bits)


def block_of_slot(slot, group_index, core, bits):
    block = group_index
    for phase in range(bits):
        if (slot >> phase) & 1:
            block = block ^ lax.shift_left(jnp.int32(1), lax.rem(jnp.int32(phase) + core, jnp.int32(bits)))
    return block


def gather_group(own, n_seq, n_heads, span):
    bits = span.bit_length() - 1
    held = own
    for phase in range(bits):
        pairs = [
            (s * n_heads + c, (s ^ order_bit(phase, c, bits)) * n_heads + c)
            for s in range(n_seq)
            for c in range(n_heads)
        ]
        got = lax.ppermute(held, ("seq", "heads"), pairs)
        held = jnp.concatenate([held, got], axis=0)
    return held


def attend(plan, info, *refs):
    (n_held, n_prev, tok, heads_step, nope, width, rank, lat, vdim, win, wpad, rows_per, span, n_docs, factor, edge) = plan
    held_refs, refs = refs[:n_held], refs[n_held:]
    prev_refs, refs = refs[:n_prev], refs[n_prev:]
    q_ref, wuk_ref, wuv_ref, o_ref, win_ref, kt_ref, j_ref, bias_ref, s0, s1, p0, p1, att_ref, sem = refs
    s_refs, p_refs = (s0, s1), (p0, p1)
    sub_tok = tok // SUBS
    rows = heads_step * sub_tok
    bits = span.bit_length() - 1
    kpad = kt_ref.shape[0]

    @pl.when(pl.program_id(0) == 0)
    def _():
        seq, core = info[0], info[1]
        place = lax.rem(seq, span)
        first = win - span * tok
        copies = []
        for turn, held in enumerate(held_refs):
            owner = lax.rem(core - turn + n_held, n_held)
            for slot in range(span):
                block = block_of_slot(slot, place, owner, bits)
                at = first + tok * lax.rem(block - place - 1 + 2 * span, span) + rows_per * owner
                at = pl.multiple_of(at, 32)
                copies.append(
                    pltpu.make_async_copy(
                        held.at[pl.ds(slot * rows_per, rows_per)], win_ref.at[pl.ds(at, rows_per)], sem.at[len(copies)]
                    )
                )
        if edge:
            lead = pltpu.make_async_copy(prev_refs[0], win_ref.at[pl.ds(0, edge)], sem.at[len(copies)])
            copies.append(lead)
        for copy in copies:
            copy.start()
        for copy in copies:
            copy.wait()
        if edge:
            at = pl.multiple_of(tok * (span - 1 - place), 32)
            copy = pltpu.make_async_copy(prev_refs[0], win_ref.at[pl.ds(at, edge)], sem.at[0])
            copy.start()
            copy.wait()
        else:
            for turn, prev in enumerate(prev_refs):
                owner = lax.rem(core - turn + n_held, n_held)
                for slot in range(span):
                    block = block_of_slot(slot, place, owner, bits)

                    @pl.when(block >= place)
                    def _():
                        at = pl.multiple_of(tok * (block - place) + rows_per * owner, 32)
                        copy = pltpu.make_async_copy(
                            prev.at[pl.ds(slot * rows_per, rows_per)], win_ref.at[pl.ds(at, rows_per)], sem.at[0]
                        )
                        copy.start()
                        copy.wait()

        for r in range(0, wpad, LANES):
            n = min(LANES, max(win - r, 0))
            if n:
                kt_ref[0:lat, r : r + n] = win_ref[r : r + n, :].T
            if n < LANES:
                kt_ref[0:lat, r + n : r + LANES] = jnp.zeros((lat, LANES - n), kt_ref.dtype)
        if kpad > lat:
            kt_ref[lat:kpad, :] = jnp.zeros((kpad - lat, wpad), kt_ref.dtype)
            j_ref[:, :, lat:kpad] = jnp.zeros((SUBS, rows, kpad - lat), j_ref.dtype)
        q_pos = seq * tok + lax.broadcasted_iota(jnp.int32, (tok, LANES), 0)
        start = jnp.zeros((tok, LANES), jnp.int32)
        end = jnp.int32(0)
        for d in range(n_docs):
            end = end + info[2 + d]
            start = jnp.where(q_pos >= end, end, start)
        for c in range(0, wpad, LANES):
            k_pos = (seq + 1) * tok - win + c + lax.broadcasted_iota(jnp.int32, (tok, LANES), 1)
            bias_ref[:, c : c + LANES] = jnp.where((k_pos >= start) & (k_pos <= q_pos), 0.0, far_negative)

    for h in range(heads_step):
        absorbed = jnp.dot(
            q_ref[:, h * width : h * width + nope], wuk_ref[h], preferred_element_type=jnp.float32
        ).astype(jnp.bfloat16)
        rope = q_ref[:, h * width + nope : (h + 1) * width]
        for g in range(SUBS):
            j_ref[g, h * sub_tok : (h + 1) * sub_tok, 0:rank] = absorbed[g * sub_tok : (g + 1) * sub_tok]
            j_ref[g, h * sub_tok : (h + 1) * sub_tok, rank:lat] = rope[g * sub_tok : (g + 1) * sub_tok]

    def reach(g):
        return win - sub_tok * (SUBS - 1 - g)

    def tiles(g):
        n = -(-reach(g) // LANES) * LANES
        return [(c, min(KEY_TILE, n - c)) for c in range(0, n, KEY_TILE)]

    def score(g):
        s_ref = s_refs[g % 2]
        top = None
        for c, w in tiles(g):
            s = jnp.dot(j_ref[g], kt_ref[:, c : c + w], preferred_element_type=jnp.float32)
            b = bias_ref[g * sub_tok : (g + 1) * sub_tok, c : c + w]
            s = (s.reshape(heads_step, sub_tok, w) + b[None]).reshape(rows, w)
            s_ref[:, c : c + w] = s
            for cc in range(0, w, LANES):
                m = s[:, cc : cc + LANES]
                top = m if top is None else jnp.maximum(top, m)
        return jnp.max(top, axis=1, keepdims=True)

    def soften(g, top):
        s_ref, p_ref = s_refs[g % 2], p_refs[g % 2]
        total = None
        for c, w in tiles(g):
            for cc in range(c, c + w, LANES):
                e = jnp.exp2((s_ref[:, cc : cc + LANES] - top) * factor)
                total = e if total is None else total + e
                p_ref[:, cc : cc + LANES] = e.astype(jnp.bfloat16)
        return jnp.sum(total, axis=1, keepdims=True)

    def mix(g, total):
        p_ref = p_refs[g % 2]
        n = reach(g)
        mixed = None
        for c in range(0, n, DOC_MOST):
            e = min(n, c + DOC_MOST)
            part = jnp.dot(p_ref[:, c:e], win_ref[c:e, 0:rank], preferred_element_type=jnp.float32)
            mixed = part if mixed is None else mixed + part
        att = (mixed * (1.0 / total)).astype(jnp.bfloat16)
        for h in range(heads_step):
            att_ref[h * tok + g * sub_tok : h * tok + (g + 1) * sub_tok, :] = att[h * sub_tok : (h + 1) * sub_tok]

    top = score(0)
    for g in range(SUBS):
        later = score(g + 1) if g + 1 < SUBS else None
        mix(g, soften(g, top))
        top = later
    for h in range(heads_step):
        o_ref[:, h * vdim : (h + 1) * vdim] = jnp.dot(
            att_ref[h * tok : (h + 1) * tok, :], wuv_ref[h], preferred_element_type=jnp.float32
        ).astype(o_ref.dtype)


def per_device(queries, latent, w_uk, w_uv, doc_lengths):
    heads_dev, nope, rank = w_uk.shape
    vdim = w_uv.shape[2]
    tok = queries.shape[0]
    width = queries.shape[1] // heads_dev
    rows_per, lat = latent.shape
    n_seq, n_heads = lax.axis_size("seq"), lax.axis_size("heads")
    span = DOC_MOST // tok
    bits = span.bit_length() - 1
    seq, core = lax.axis_index("seq"), lax.axis_index("heads")

    held = gather_group(latent, n_seq, n_heads, span)
    turned = [held]
    for turn in range(1, n_heads):
        turned.append(lax.ppermute(held, "heads", [(c, (c + turn) % n_heads) for c in range(n_heads)]))

    if n_seq == 2 * span:
        edge = TAIL_MOST
        win = DOC_MOST + edge
        place = lax.rem(seq, span)
        slot = jnp.int32(0)
        for s in range(span):
            slot = jnp.where(block_of_slot(s, place, core, bits) == span - 1, s, slot)
        edge_rows = lax.dynamic_slice_in_dim(held, (slot + 1) * rows_per - edge, edge, 0)
        prev = None
        for c in range(n_heads):
            pairs = [(s * n_heads + n_heads - 1, (s + span) * n_heads + c) for s in range(span)]
            got = lax.ppermute(edge_rows, ("seq", "heads"), pairs)
            prev = got if prev is None else jnp.where(core == c, got, prev)
        prev = [prev]
    else:
        edge = 0
        win = DOC_MOST + tok
        prev = [lax.ppermute(t, "seq", [(s, s + span) for s in range(n_seq - span)]) for t in turned]

    info = jnp.concatenate([jnp.stack([seq, core]).astype(jnp.int32), doc_lengths])
    step = min(HEADS_STEP, heads_dev)
    wpad = -(-win // KEY_TILE) * KEY_TILE
    kpad = -(-lat // LANES) * LANES
    rows = step * tok // SUBS
    plan = (
        len(turned), len(prev), tok, step, nope, width, rank, lat, vdim, win, wpad, rows_per, span,
        doc_lengths.shape[0], width**-0.5 * math.log2(math.e), edge,
    )
    hbm = pl.BlockSpec(memory_space=pl.ANY)
    return pl.pallas_call(
        functools.partial(attend, plan),
        grid=(heads_dev // step,),
        in_specs=[pl.BlockSpec(memory_space=pltpu.SMEM)]
        + [hbm] * (len(turned) + len(prev))
        + [
            pl.BlockSpec((tok, step * width), lambda i: (0, i)),
            pl.BlockSpec((step, nope, rank), lambda i: (i, 0, 0)),
            pl.BlockSpec((step, rank, vdim), lambda i: (i, 0, 0)),
        ],
        out_specs=pl.BlockSpec((tok, step * vdim), lambda i: (0, i)),
        out_shape=jax.ShapeDtypeStruct((tok, heads_dev * vdim), jnp.bfloat16),
        scratch_shapes=[
            pltpu.VMEM((win, lat), jnp.bfloat16),
            pltpu.VMEM((kpad, wpad), jnp.bfloat16),
            pltpu.VMEM((SUBS, rows, kpad), jnp.bfloat16),
            pltpu.VMEM((tok, wpad), jnp.float32),
            pltpu.VMEM((rows, wpad), jnp.float32),
            pltpu.VMEM((rows, wpad), jnp.float32),
            pltpu.VMEM((rows, wpad), jnp.bfloat16),
            pltpu.VMEM((rows, wpad), jnp.bfloat16),
            pltpu.VMEM((step * tok, rank), jnp.bfloat16),
            pltpu.SemaphoreType.DMA((span * len(turned) + 1,)),
        ],
        compiler_params=pltpu.CompilerParams(vmem_limit_bytes=32 * 1024 * 1024),
    )(info, *turned, *prev, queries, w_uk, w_uv)


def solution(mesh):
    return jax.shard_map(
        per_device,
        mesh=mesh,
        in_specs=(
            P("seq", "heads"),
            P(("seq", "heads"), None),
            P("heads", None, None),
            P("heads", None, None),
            P(),
        ),
        out_specs=P("seq", "heads"),
        check_vma=False,
    )
```

```python
import functools
import math

import jax
import jax.numpy as jnp
from jax import lax
from jax.experimental import pallas as pl
from jax.experimental.pallas import tpu as pltpu
from jax.sharding import PartitionSpec as P

DOC_MOST = 1024
TAIL_MOST = 32
SUBS = 4
KEY_TILE = 256
LANES = 128
HEADS_GROUP = 8
HEADS_STEP = 16

far_negative = -1e30


def absorb(tok, nope, width, rank, lat, q_ref, wuk_ref, wuv_hbm, j_ref, wuv_ref, sem):
    step = pl.program_id(0)
    sub_tok = tok // SUBS
    rows = j_ref.shape[2]
    group = rows // sub_tok
    groups_step = wuk_ref.shape[0] // group
    kpad = j_ref.shape[3]
    copy = pltpu.make_async_copy(wuv_hbm, wuv_ref, sem)

    @pl.when(step == 0)
    def _():
        copy.start()

    for h in range(wuk_ref.shape[0]):
        absorbed = jnp.dot(
            q_ref[:, h * width : h * width + nope], wuk_ref[h], preferred_element_type=jnp.float32
        ).astype(jnp.bfloat16)
        rope = q_ref[:, h * width + nope : (h + 1) * width]
        if kpad > lat:
            rope = jnp.concatenate([rope, jnp.zeros((tok, kpad - lat), rope.dtype)], axis=1)
        i = step * groups_step + h // group
        at = (h % group) * sub_tok
        for g in range(SUBS):
            j_ref[i, g, at : at + sub_tok, 0:rank] = absorbed[g * sub_tok : (g + 1) * sub_tok]
            j_ref[i, g, at : at + sub_tok, rank:kpad] = rope[g * sub_tok : (g + 1) * sub_tok]

    @pl.when(step == pl.num_programs(0) - 1)
    def _():
        copy.wait()


def attend(plan, info, *refs):
    (n_heads, tok, rank, lat, vdim, win, wpad, span, n_docs, factor) = plan
    per = -(-span // n_heads)
    own, refs = refs[0], refs[1:]
    pieces, refs = refs[: per * n_heads], refs[per * n_heads :]
    j_ref, wuv_ref, o_ref, win_ref, kt_ref, bias_ref, s0, s1, p0, p1, att_ref = refs
    s_refs, p_refs = (s0, s1), (p0, p1)
    sub_tok = tok // SUBS
    n_groups, _, rows, kpad = j_ref.shape
    group = rows // sub_tok

    seq, core = info[0], info[1]
    lead = win - span * tok
    win_ref[win - tok : win, :] = own[...]
    for turn in range(n_heads):
        owner = lax.rem(core - turn + n_heads, n_heads)
        for n in range(per):
            piece = pieces[turn * per + n]
            shift = 1 + owner * per + n
            if lead == tok:
                at = tok * (span - shift)
                win_ref[pl.ds(pl.multiple_of(at, tok), tok), :] = piece[...]
            else:
                at = jnp.maximum(lead + tok * (span - 1 - shift), 0)
                is_last = shift == span
                part = jnp.where(is_last, piece[tok - lead : tok, :], piece[0:lead, :])
                win_ref[pl.ds(pl.multiple_of(at, lead), lead), :] = part
                at = jnp.where(is_last, win, at + lead)
                win_ref[pl.ds(pl.multiple_of(at, lead), tok - lead), :] = piece[lead:tok, :]
    q_pos = seq * tok + lax.broadcasted_iota(jnp.int32, (tok, LANES), 0)
    start = jnp.zeros((tok, LANES), jnp.int32)
    end = jnp.int32(0)
    for d in range(n_docs):
        end = end + info[2 + d]
        start = jnp.where(q_pos >= end, end, start)
    for c in range(0, wpad, LANES):
        k_pos = (seq + 1) * tok - win + c + lax.broadcasted_iota(jnp.int32, (tok, LANES), 1)
        bias_ref[:, c : c + LANES] = jnp.where((k_pos >= start) & (k_pos <= q_pos), 0.0, far_negative)

    for r in range(0, wpad, LANES):
        n = min(LANES, max(win - r, 0))
        if n:
            kt_ref[0:lat, r : r + n] = win_ref[r : r + n, :].T
        if n < LANES:
            kt_ref[0:lat, r + n : r + LANES] = jnp.zeros((lat, LANES - n), kt_ref.dtype)
    if kpad > lat:
        kt_ref[lat:kpad, :] = jnp.zeros((kpad - lat, wpad), kt_ref.dtype)

    def reach(g):
        return win - sub_tok * (SUBS - 1 - g)

    def tiles(g):
        n = -(-reach(g) // LANES) * LANES
        return [(c, min(KEY_TILE, n - c)) for c in range(0, n, KEY_TILE)]

    def score(i, g):
        s_ref = s_refs[g % 2]
        top = None
        for c, w in tiles(g):
            s = jnp.dot(j_ref[i, g], kt_ref[:, c : c + w], preferred_element_type=jnp.float32)
            b = bias_ref[g * sub_tok : (g + 1) * sub_tok, c : c + w]
            s = (s.reshape(group, sub_tok, w) + b[None]).reshape(rows, w)
            s_ref[:, c : c + w] = s
            for cc in range(0, w, LANES):
                m = s[:, cc : cc + LANES]
                top = m if top is None else jnp.maximum(top, m)
        return jnp.max(top, axis=1, keepdims=True)

    def soften(g, top):
        s_ref, p_ref = s_refs[g % 2], p_refs[g % 2]
        total = None
        for c, w in tiles(g):
            for cc in range(c, c + w, LANES):
                e = jnp.exp2((s_ref[:, cc : cc + LANES] - top) * factor)
                total = e if total is None else total + e
                p_ref[:, cc : cc + LANES] = e.astype(jnp.bfloat16)
        return jnp.sum(total, axis=1, keepdims=True)

    def mix(g, total):
        p_ref = p_refs[g % 2]
        n = reach(g)
        mixed = None
        for c in range(0, n, DOC_MOST):
            e = min(n, c + DOC_MOST)
            part = jnp.dot(p_ref[:, c:e], win_ref[c:e, 0:rank], preferred_element_type=jnp.float32)
            mixed = part if mixed is None else mixed + part
        att = (mixed * (1.0 / total)).astype(jnp.bfloat16)
        for h in range(group):
            att_ref[h * tok + g * sub_tok : h * tok + (g + 1) * sub_tok, :] = att[h * sub_tok : (h + 1) * sub_tok]

    def one_group(i, top):
        for g in range(SUBS):
            if g + 1 < SUBS:
                later = score(i, g + 1)
            else:
                later = score(jnp.minimum(i + 1, n_groups - 1), 0)
            mix(g, soften(g, top))
            top = later
        for h in range(group):
            out = jnp.dot(
                att_ref[h * tok : (h + 1) * tok, :], wuv_ref[i * group + h], preferred_element_type=jnp.float32
            ).astype(o_ref.dtype)
            at = pl.multiple_of((i * group + h) * vdim, vdim)
            o_ref[:, pl.ds(at, vdim)] = out
        return top

    lax.fori_loop(0, n_groups, one_group, score(0, 0))


def near(arrays):
    return [pltpu.with_memory_space_constraint(x, pltpu.VMEM) for x in arrays]


def far(arrays):
    return [pltpu.with_memory_space_constraint(x, pltpu.HBM) for x in arrays]


def per_device(queries, latent, w_uk, w_uv, doc_lengths):
    heads_dev, nope, rank = w_uk.shape
    vdim = w_uv.shape[2]
    tok = queries.shape[0]
    width = queries.shape[1] // heads_dev
    rows_per, lat = latent.shape
    n_seq, n_heads = lax.axis_size("seq"), lax.axis_size("heads")
    span = DOC_MOST // tok
    seq, core = lax.axis_index("seq"), lax.axis_index("heads")
    group = min(HEADS_GROUP, heads_dev)
    step = min(HEADS_STEP, heads_dev)
    rows = group * tok // SUBS
    kpad = -(-lat // LANES) * LANES

    per = -(-span // n_heads)
    far_block = n_seq - span - 1

    def asked(source, target):
        return source >= 0 and (target < n_seq - span or source >= far_block)

    win = DOC_MOST + (TAIL_MOST if n_seq == 2 * span else tok)
    own = lax.all_gather(latent, "heads", axis=0, tiled=True)
    info = jnp.concatenate([jnp.stack([seq, core]).astype(jnp.int32), doc_lengths])
    direct = []
    for n in range(per):
        pairs = []
        for c in range(n_heads):
            shift = 1 + c * per + n
            if shift <= span:
                pairs += [
                    ((t - shift) * n_heads + c, t * n_heads + c) for t in range(n_seq) if asked(t - shift, t)
                ]
        direct.append(lax.ppermute(own, ("seq", "heads"), pairs))
    own, info, queries = lax.optimization_barrier((own, info, queries))

    hbm = pl.BlockSpec(memory_space=pl.ANY)
    vmem = pl.BlockSpec(memory_space=pltpu.VMEM)
    j_shape = (heads_dev // group, SUBS, rows, kpad)
    joined, w_uv_near = pl.pallas_call(
        functools.partial(absorb, tok, nope, width, rank, lat),
        grid=(heads_dev // step,),
        in_specs=[
            pl.BlockSpec((tok, step * width), lambda i: (0, i)),
            pl.BlockSpec((step, nope, rank), lambda i: (i, 0, 0)),
            hbm,
        ],
        out_specs=[vmem, vmem],
        out_shape=[pltpu.VMEM(j_shape, jnp.bfloat16), pltpu.VMEM(w_uv.shape, w_uv.dtype)],
        scratch_shapes=[pltpu.SemaphoreType.DMA],
        compiler_params=pltpu.CompilerParams(vmem_limit_bytes=24 * 1024 * 1024),
        cost_estimate=pl.CostEstimate(
            flops=2 * tok * heads_dev * nope * rank, bytes_accessed=2 * (w_uk.size + w_uv.size + queries.size), transcendentals=0
        ),
    )(*far([queries, w_uk, w_uv]))
    direct, joined, w_uv_near = lax.optimization_barrier((direct, joined, w_uv_near))

    pieces = list(direct)
    for turn in range(1, n_heads):
        pairs = [(c, (c + turn) % n_heads) for c in range(n_heads)]
        pieces += [lax.ppermute(x, "heads", pairs) for x in direct]

    wpad = -(-win // KEY_TILE) * KEY_TILE
    plan = (
        n_heads, tok, rank, lat, vdim, win, wpad, span, doc_lengths.shape[0], width**-0.5 * math.log2(math.e),
    )
    return pl.pallas_call(
        functools.partial(attend, plan),
        in_specs=[pl.BlockSpec(memory_space=pltpu.SMEM)] + [vmem] * (len(pieces) + 3),
        out_specs=vmem,
        out_shape=jax.ShapeDtypeStruct((tok, heads_dev * vdim), jnp.bfloat16),
        scratch_shapes=[
            pltpu.VMEM((win + tok, lat), jnp.bfloat16),
            pltpu.VMEM((kpad, wpad), jnp.bfloat16),
            pltpu.VMEM((tok, wpad), jnp.float32),
            pltpu.VMEM((rows, wpad), jnp.float32),
            pltpu.VMEM((rows, wpad), jnp.float32),
            pltpu.VMEM((rows, wpad), jnp.bfloat16),
            pltpu.VMEM((rows, wpad), jnp.bfloat16),
            pltpu.VMEM((group * tok, rank), jnp.bfloat16),
        ],
        compiler_params=pltpu.CompilerParams(vmem_limit_bytes=24 * 1024 * 1024),
    )(info, *near([own, *pieces, joined, w_uv_near]))


def solution(mesh):
    return jax.shard_map(
        per_device,
        mesh=mesh,
        in_specs=(
            P("seq", "heads"),
            P(("seq", "heads"), None),
            P("heads", None, None),
            P("heads", None, None),
            P(),
        ),
        out_specs=P("seq", "heads"),
        check_vma=False,
    )
```

```python
import functools
import math

import jax
import jax.numpy as jnp
from jax import lax
from jax.experimental import pallas as pl
from jax.experimental.pallas import tpu as pltpu
from jax.sharding import PartitionSpec as P

DOC_MOST = 1024
TAIL_MOST = 32
SUBS = 4
KEY_TILE = 256
LANES = 128
HEADS_GROUP = 8
HEADS_STEP = 16
PARTS = (1, 3)
LIGHT_TILES = 2

far_negative = -1e30


def absorb(tok, nope, width, rank, lat, base, first, brings, *refs):
    step = pl.program_id(0)
    q_ref, wuk_ref, refs = refs[0], refs[1], refs[2:]
    if not first:
        refs = refs[1:]
    if brings:
        wuv_hbm, j_ref, wuv_ref, sem = refs
        copy = pltpu.make_async_copy(wuv_hbm, wuv_ref, sem)

        @pl.when(step == 0)
        def _():
            copy.start()
    else:
        (j_ref,) = refs
    sub_tok = tok // SUBS
    rows = j_ref.shape[2]
    group = rows // sub_tok
    groups_step = wuk_ref.shape[0] // group
    kpad = j_ref.shape[3]

    for h in range(wuk_ref.shape[0]):
        absorbed = jnp.dot(
            q_ref[:, h * width : h * width + nope], wuk_ref[h], preferred_element_type=jnp.float32
        ).astype(jnp.bfloat16)
        rope = q_ref[:, h * width + nope : (h + 1) * width]
        if kpad > lat:
            rope = jnp.concatenate([rope, jnp.zeros((tok, kpad - lat), rope.dtype)], axis=1)
        i = (base + step) * groups_step + h // group
        at = (h % group) * sub_tok
        for g in range(SUBS):
            j_ref[i, g, at : at + sub_tok, 0:rank] = absorbed[g * sub_tok : (g + 1) * sub_tok]
            j_ref[i, g, at : at + sub_tok, rank:kpad] = rope[g * sub_tok : (g + 1) * sub_tok]

    if brings:

        @pl.when(step == pl.num_programs(0) - 1)
        def _():
            copy.wait()


def pack(n_heads, edge, *refs):
    o_ref = refs[-1]
    core = lax.axis_index("heads")
    rows_per = refs[0].shape[0]
    for turn in range(n_heads):
        owner = lax.rem(core - turn + n_heads, n_heads)
        o_ref[pl.ds(pl.multiple_of(rows_per * owner, rows_per), rows_per), :] = refs[turn][...]
    if edge:
        rows = refs[n_heads][rows_per - edge :, :]
        for c in range(1, n_heads):
            rows = jnp.where(core == c, refs[n_heads + c][rows_per - edge :, :], rows)
        o_ref[rows_per * n_heads :, :] = rows


def partners(span, n_heads):
    ks = sorted(range(1, span), key=lambda k: (k.bit_count(), k))
    per = -(-len(ks) // n_heads)
    ks += [0] * (per * n_heads - len(ks))
    return [ks[n * n_heads : (n + 1) * n_heads] for n in range(per)]


def attend(plan, lengths, *refs):
    (n_heads, tok, rank, lat, vdim, win, wpad, span, n_docs, factor, edge) = plan
    per = -(-(span - 1 if edge else span) // n_heads)
    own, refs = refs[0], refs[1:]
    pieces, refs = refs[: per * n_heads], refs[per * n_heads :]
    j_ref, wuv_ref, o_ref, win_ref, kt_ref, bias_ref, s0, s1, p0, p1, att_ref = refs
    s_refs, p_refs = (s0, s1), (p0, p1)
    sub_tok = tok // SUBS
    n_groups, _, rows, kpad = j_ref.shape
    group = rows // sub_tok

    seq, core = lax.axis_index("seq"), lax.axis_index("heads")
    if edge:
        place = lax.rem(seq, span)
        held = [(own, place, place)]
        for turn in range(n_heads):
            owner = lax.rem(core - turn + n_heads, n_heads)
            for n, ks in enumerate(partners(span, n_heads)):
                k = jnp.int32(0)
                for c, kc in enumerate(ks):
                    k = jnp.where(owner == c, kc, k)
                block = lax.bitwise_xor(place, k)
                held.append((pieces[turn * per + n], block, jnp.where(k == 0, span, block)))
        for piece, block, _ in held[1:] + held[:1]:
            at = edge + tok * lax.rem(block - place - 1 + 2 * span, span)
            win_ref[pl.ds(pl.multiple_of(at, edge), tok), :] = piece[0:tok, :]
        win_ref[0:edge, :] = own[0:edge, :]
        for piece, _, block in held:
            at = jnp.where(block == span // 2 - 1, tok * (span - 1 - place), win)
            win_ref[pl.ds(pl.multiple_of(at, edge), edge), :] = piece[tok : tok + edge, :]
    else:
        win_ref[win - tok : win, :] = own[...]
        for turn in range(n_heads):
            owner = lax.rem(core - turn + n_heads, n_heads)
            for n in range(per):
                at = tok * (span - 1 - owner * per - n)
                win_ref[pl.ds(pl.multiple_of(at, tok), tok), :] = pieces[turn * per + n][...]
    q_pos = seq * tok + lax.broadcasted_iota(jnp.int32, (tok, LANES), 0)
    start = jnp.zeros((tok, LANES), jnp.int32)
    end = jnp.int32(0)
    for d in range(n_docs):
        end = end + lengths[d]
        start = jnp.where(q_pos >= end, end, start)
    for c in range(0, wpad, LANES):
        k_pos = (seq + 1) * tok - win + c + lax.broadcasted_iota(jnp.int32, (tok, LANES), 1)
        bias_ref[:, c : c + LANES] = jnp.where((k_pos >= start) & (k_pos <= q_pos), 0.0, far_negative)

    for r in range(0, wpad, LANES):
        n = min(LANES, max(win - r, 0))
        if n:
            kt_ref[0:lat, r : r + n] = win_ref[r : r + n, :].T
        if n < LANES:
            kt_ref[0:lat, r + n : r + LANES] = jnp.zeros((lat, LANES - n), kt_ref.dtype)
    if kpad > lat:
        kt_ref[lat:kpad, :] = jnp.zeros((kpad - lat, wpad), kt_ref.dtype)

    def groups_from(skip):
        def reach(g):
            return win - sub_tok * (SUBS - 1 - g)

        def tiles(g):
            n = -(-reach(g) // LANES) * LANES
            return [(c, min(KEY_TILE, n - c)) for c in range(skip, n, KEY_TILE)]

        def score(i, g):
            s_ref = s_refs[g % 2]
            top = None
            for c, w in tiles(g):
                s = jnp.dot(j_ref[i, g], kt_ref[:, c : c + w], preferred_element_type=jnp.float32)
                b = bias_ref[g * sub_tok : (g + 1) * sub_tok, c : c + w]
                s = (s.reshape(group, sub_tok, w) + b[None]).reshape(rows, w)
                s_ref[:, c : c + w] = s
                for cc in range(0, w, LANES):
                    m = s[:, cc : cc + LANES]
                    top = m if top is None else jnp.maximum(top, m)
            return jnp.max(top, axis=1, keepdims=True)

        def soften(g, top):
            s_ref, p_ref = s_refs[g % 2], p_refs[g % 2]
            total = None
            for c, w in tiles(g):
                for cc in range(c, c + w, LANES):
                    e = jnp.exp2((s_ref[:, cc : cc + LANES] - top) * factor)
                    total = e if total is None else total + e
                    p_ref[:, cc : cc + LANES] = e.astype(jnp.bfloat16)
            return jnp.sum(total, axis=1, keepdims=True)

        def mix(g, total):
            p_ref = p_refs[g % 2]
            n = reach(g)
            mixed = None
            for c in range(skip, n, DOC_MOST - skip):
                e = min(n, c + DOC_MOST - skip)
                part = jnp.dot(p_ref[:, c:e], win_ref[c:e, 0:rank], preferred_element_type=jnp.float32)
                mixed = part if mixed is None else mixed + part
            att = (mixed * (1.0 / total)).astype(jnp.bfloat16)
            for h in range(group):
                att_ref[h * tok + g * sub_tok : h * tok + (g + 1) * sub_tok, :] = att[h * sub_tok : (h + 1) * sub_tok]

        def one_group(i, top):
            for g in range(SUBS):
                if g + 1 < SUBS:
                    later = score(i, g + 1)
                else:
                    later = score(jnp.minimum(i + 1, n_groups - 1), 0)
                mix(g, soften(g, top))
                top = later
            for h in range(group):
                out = jnp.dot(
                    att_ref[h * tok : (h + 1) * tok, :], wuv_ref[i * group + h], preferred_element_type=jnp.float32
                ).astype(o_ref.dtype)
                at = pl.multiple_of((i * group + h) * vdim, vdim)
                o_ref[:, pl.ds(at, vdim)] = out
            return top

        lax.fori_loop(0, n_groups, one_group, score(0, 0))

    block_start, end = jnp.int32(0), jnp.int32(0)
    for d in range(n_docs):
        end = end + lengths[d]
        block_start = jnp.where(seq * tok >= end, end, block_start)
    low = block_start - ((seq + 1) * tok - win)
    for tiles_out in range(LIGHT_TILES + 1):
        least = low >= tiles_out * KEY_TILE
        most = low < (tiles_out + 1) * KEY_TILE
        if tiles_out == 0:
            taken = most
        elif tiles_out == LIGHT_TILES:
            taken = least
        else:
            taken = least & most

        @pl.when(taken)
        def _(skip=tiles_out * KEY_TILE):
            groups_from(skip)


def near(arrays):
    return [pltpu.with_memory_space_constraint(x, pltpu.VMEM) for x in arrays]


def far(arrays):
    return [pltpu.with_memory_space_constraint(x, pltpu.HBM) for x in arrays]


def per_device(queries, latent, w_uk, w_uv, doc_lengths):
    heads_dev, nope, rank = w_uk.shape
    vdim = w_uv.shape[2]
    tok = queries.shape[0]
    width = queries.shape[1] // heads_dev
    rows_per, lat = latent.shape
    n_seq, n_heads = lax.axis_size("seq"), lax.axis_size("heads")
    span = DOC_MOST // tok
    group = min(HEADS_GROUP, heads_dev)
    step = min(HEADS_STEP, heads_dev)
    rows = group * tok // SUBS
    kpad = -(-lat // LANES) * LANES

    edge = TAIL_MOST if n_seq == 2 * span else 0
    win = DOC_MOST + (edge or tok)
    hbm = pl.BlockSpec(memory_space=pl.ANY)
    vmem = pl.BlockSpec(memory_space=pltpu.VMEM)
    joined_type = pltpu.VMEM((heads_dev // group, SUBS, rows, kpad), jnp.bfloat16)
    steps = heads_dev // step

    def absorb_call(part, joined, brings):
        base = steps * sum(PARTS[:part]) // sum(PARTS)
        count = steps * sum(PARTS[: part + 1]) // sum(PARTS) - base
        heads = count * step
        wuv_type = pltpu.VMEM(w_uv.shape, w_uv.dtype)
        return pl.pallas_call(
            functools.partial(absorb, tok, nope, width, rank, lat, base, joined is None, brings),
            grid=(count,),
            in_specs=[
                pl.BlockSpec((tok, step * width), lambda i: (0, base + i)),
                pl.BlockSpec((step, nope, rank), lambda i: (base + i, 0, 0)),
            ]
            + [vmem] * (joined is not None)
            + [hbm] * brings,
            out_specs=[vmem] * (1 + brings),
            out_shape=[joined_type] + [wuv_type] * brings,
            scratch_shapes=[pltpu.SemaphoreType.DMA] * brings,
            compiler_params=pltpu.CompilerParams(vmem_limit_bytes=24 * 1024 * 1024),
            cost_estimate=pl.CostEstimate(
                flops=2 * tok * heads * nope * rank, bytes_accessed=4 * heads * nope * rank, transcendentals=0
            ),
            input_output_aliases={} if joined is None else {2: 0},
        )(*far([queries, w_uk]), *([] if joined is None else near([joined])), *far([w_uv] * brings))

    def swap(x, turn):
        return lax.ppermute(x, "heads", [(c, (c + turn) % n_heads) for c in range(n_heads)])

    bits = [latent] + [swap(latent, turn) for turn in range(1, n_heads)]
    if edge:
        source = span * n_heads - 1
        target = (span + span // 2 - 1) * n_heads
        bits += [lax.ppermute(latent, ("seq", "heads"), [(source, target + c)]) for c in range(n_heads)]
    (joined,) = absorb_call(0, None, False)
    *bits, joined = lax.optimization_barrier((*bits, joined))
    own = pl.pallas_call(
        functools.partial(pack, n_heads, edge),
        in_specs=[vmem] * len(bits),
        out_specs=vmem,
        out_shape=pltpu.VMEM((tok + edge, lat), latent.dtype),
        compiler_params=pltpu.CompilerParams(vmem_limit_bytes=2 * 1024 * 1024),
    )(*near(bits))
    direct = []
    if edge:
        for ks in partners(span, n_heads):
            pairs = [
                (t * n_heads + c, (t ^ k) * n_heads + c) for c, k in enumerate(ks) if k for t in range(n_seq)
            ]
            direct.append(lax.ppermute(own, ("seq", "heads"), pairs))
    else:
        per = -(-span // n_heads)
        for n in range(per):
            pairs = []
            for c in range(n_heads):
                shift = 1 + c * per + n
                if shift <= span:
                    pairs += [(t * n_heads + c, (t + shift) * n_heads + c) for t in range(n_seq - shift)]
            direct.append(lax.ppermute(own, ("seq", "heads"), pairs))
    own, joined = lax.optimization_barrier((own, joined))
    joined, w_uv_near = absorb_call(1, joined, True)
    *direct, joined = lax.optimization_barrier((*direct, joined))
    pieces = list(direct)
    for turn in range(1, n_heads):
        pieces += [swap(x, turn) for x in direct]
    if len(PARTS) > 2:
        (joined,) = absorb_call(2, joined, False)

    wpad = -(-win // KEY_TILE) * KEY_TILE
    plan = (
        n_heads, tok, rank, lat, vdim, win, wpad, span, doc_lengths.shape[0], width**-0.5 * math.log2(math.e),
        edge,
    )
    return pl.pallas_call(
        functools.partial(attend, plan),
        in_specs=[pl.BlockSpec(memory_space=pltpu.SMEM)] + [vmem] * (len(pieces) + 3),
        out_specs=vmem,
        out_shape=jax.ShapeDtypeStruct((tok, heads_dev * vdim), jnp.bfloat16),
        scratch_shapes=[
            pltpu.VMEM((win + tok, lat), jnp.bfloat16),
            pltpu.VMEM((kpad, wpad), jnp.bfloat16),
            pltpu.VMEM((tok, wpad), jnp.float32),
            pltpu.VMEM((rows, wpad), jnp.float32),
            pltpu.VMEM((rows, wpad), jnp.float32),
            pltpu.VMEM((rows, wpad), jnp.bfloat16),
            pltpu.VMEM((rows, wpad), jnp.bfloat16),
            pltpu.VMEM((group * tok, rank), jnp.bfloat16),
        ],
        compiler_params=pltpu.CompilerParams(vmem_limit_bytes=24 * 1024 * 1024),
    )(doc_lengths, *near([own, *pieces, joined, w_uv_near]))


def solution(mesh):
    return jax.shard_map(
        per_device,
        mesh=mesh,
        in_specs=(
            P("seq", "heads"),
            P(("seq", "heads"), None),
            P("heads", None, None),
            P("heads", None, None),
            P(),
        ),
        out_specs=P("seq", "heads"),
        check_vma=False,
    )
```

```python
import functools
import math

import jax
import jax.numpy as jnp
from jax import lax
from jax.experimental import pallas as pl
from jax.experimental.pallas import tpu as pltpu
from jax.sharding import PartitionSpec as P

DOC_MOST = 1024
TAIL_MOST = 32
SUBS = 4
KEY_TILE = 256
LANES = 128
HEADS_GROUP = 8
HEADS_STEP = 16
PARTS = (1, 3)
LIGHT_TILES = 2
OUT_PARTS = 4
SOFT_ROWS = 16

far_negative = -1e30


def absorb(tok, nope, width, rank, lat, base, *refs):
    step = pl.program_id(0)
    q_ref, wuk_ref, j_ref = refs[0], refs[1], refs[-1]
    sub_tok = tok // SUBS
    rows = j_ref.shape[2]
    group = rows // sub_tok
    groups_step = wuk_ref.shape[0] // group
    kpad = j_ref.shape[3]

    for h in range(wuk_ref.shape[0]):
        absorbed = jnp.dot(
            q_ref[:, h * width : h * width + nope], wuk_ref[h], preferred_element_type=jnp.float32
        ).astype(jnp.bfloat16)
        rope = q_ref[:, h * width + nope : (h + 1) * width]
        if kpad > lat:
            rope = jnp.concatenate([rope, jnp.zeros((tok, kpad - lat), rope.dtype)], axis=1)
        i = (base + step) * groups_step + h // group
        at = (h % group) * sub_tok
        for g in range(SUBS):
            j_ref[i, g, at : at + sub_tok, 0:rank] = absorbed[g * sub_tok : (g + 1) * sub_tok]
            j_ref[i, g, at : at + sub_tok, rank:kpad] = rope[g * sub_tok : (g + 1) * sub_tok]


def pack(n_heads, edge, *refs):
    o_ref = refs[-1]
    core = lax.axis_index("heads")
    rows_per = refs[0].shape[0]
    for turn in range(n_heads):
        owner = lax.rem(core - turn + n_heads, n_heads)
        o_ref[pl.ds(pl.multiple_of(rows_per * owner, rows_per), rows_per), :] = refs[turn][...]
    if edge:
        rows = refs[n_heads][rows_per - edge :, :]
        for c in range(1, n_heads):
            rows = jnp.where(core == c, refs[n_heads + c][rows_per - edge :, :], rows)
        o_ref[rows_per * n_heads :, :] = rows


def partners(span, n_heads):
    ks = sorted(range(1, span), key=lambda k: (-k.bit_count(), k))
    per = -(-len(ks) // n_heads)
    ks += [0] * (per * n_heads - len(ks))
    return [ks[n * n_heads : (n + 1) * n_heads] for n in range(per)]


def attend(plan, lengths, *refs):
    (n_heads, tok, rank, lat, vdim, win, wpad, span, n_docs, factor, edge) = plan
    per = -(-(span - 1 if edge else span) // n_heads)
    own, refs = refs[0], refs[1:]
    pieces, refs = refs[: per * n_heads], refs[per * n_heads :]
    j_ref, wuv_hbm, o_hbm, win_ref, kt_ref, bias_ref, s0, s1, p0, p1, att_ref, wuv_ref, o_ref, sem = refs
    s_refs, p_refs = (s0, s1), (p0, p1)
    sub_tok = tok // SUBS
    n_groups, _, rows, kpad = j_ref.shape
    group = rows // sub_tok

    wuv_copy = pltpu.make_async_copy(wuv_hbm, wuv_ref, sem.at[0])
    wuv_copy.start()
    seq, core = lax.axis_index("seq"), lax.axis_index("heads")
    win_ref[win:, :] = jnp.zeros((win_ref.shape[0] - win, lat), win_ref.dtype)
    if edge:
        place = lax.rem(seq, span)
        held = [(own, place, place)]
        for turn in range(n_heads):
            owner = lax.rem(core - turn + n_heads, n_heads)
            for n, ks in enumerate(partners(span, n_heads)):
                k = jnp.int32(0)
                for c, kc in enumerate(ks):
                    k = jnp.where(owner == c, kc, k)
                block = lax.bitwise_xor(place, k)
                held.append((pieces[turn * per + n], block, jnp.where(k == 0, span, block)))
        for piece, block, _ in held[1:] + held[:1]:
            at = edge + tok * lax.rem(block - place - 1 + 2 * span, span)
            win_ref[pl.ds(pl.multiple_of(at, edge), tok), :] = piece[0:tok, :]
        win_ref[0:edge, :] = own[0:edge, :]
        for piece, _, block in held:
            at = jnp.where(block == span // 2 - 1, tok * (span - 1 - place), win)
            win_ref[pl.ds(pl.multiple_of(at, edge), edge), :] = piece[tok : tok + edge, :]
    else:
        win_ref[win - tok : win, :] = own[...]
        for turn in range(n_heads):
            owner = lax.rem(core - turn + n_heads, n_heads)
            for n in range(per):
                at = tok * (span - 1 - owner * per - n)
                win_ref[pl.ds(pl.multiple_of(at, tok), tok), :] = pieces[turn * per + n][...]
    q_pos = seq * tok + lax.broadcasted_iota(jnp.int32, (tok, LANES), 0)
    start = jnp.zeros((tok, LANES), jnp.int32)
    end = jnp.int32(0)
    for d in range(n_docs):
        end = end + lengths[d]
        start = jnp.where(q_pos >= end, end, start)
    for c in range(0, wpad, LANES):
        k_pos = (seq + 1) * tok - win + c + lax.broadcasted_iota(jnp.int32, (tok, LANES), 1)
        bias_ref[:, c : c + LANES] = jnp.where((k_pos >= start) & (k_pos <= q_pos), 0.0, far_negative)

    for r in range(0, wpad, LANES):
        n = min(LANES, max(win - r, 0))
        if n:
            kt_ref[0:lat, r : r + n] = win_ref[r : r + n, :].T
        if n < LANES:
            kt_ref[0:lat, r + n : r + LANES] = jnp.zeros((lat, LANES - n), kt_ref.dtype)
    if kpad > lat:
        kt_ref[lat:kpad, :] = jnp.zeros((kpad - lat, wpad), kt_ref.dtype)

    def groups_from(skip):
        def reach(g):
            return win - sub_tok * (SUBS - 1 - g)

        def tiles(g):
            n = -(-reach(g) // LANES) * LANES
            return [(c, min(KEY_TILE, n - c)) for c in range(skip, n, KEY_TILE)]

        def score(i, g):
            for c, w in tiles(g):
                s = jnp.dot(j_ref[i, g], kt_ref[:, c : c + w], preferred_element_type=jnp.float32)
                b = bias_ref[g * sub_tok : (g + 1) * sub_tok, c : c + w]
                s_refs[g % 2][:, c : c + w] = (s.reshape(group, sub_tok, w) + b[None]).reshape(rows, w)

        def soften(g):
            s_ref, p_ref = s_refs[g % 2], p_refs[g % 2]
            columns = [slice(cc, cc + LANES) for c, w in tiles(g) for cc in range(c, c + w, LANES)]
            totals = []
            for r in range(0, rows, SOFT_ROWS):
                s = [s_ref[r : r + SOFT_ROWS, at] for at in columns]
                top = jnp.max(functools.reduce(jnp.maximum, s), axis=1, keepdims=True)
                e = [jnp.exp2((x - top) * factor) for x in s]
                totals.append(jnp.sum(functools.reduce(jnp.add, e), axis=1, keepdims=True))
                for at, x in zip(columns, e):
                    p_ref[r : r + SOFT_ROWS, at] = x.astype(jnp.bfloat16)
            return totals

        def mix(i, g, totals):
            n = tiles(g)[-1][0] + tiles(g)[-1][1]
            mixed = jnp.dot(p_refs[g % 2][:, skip:n], win_ref[skip:n, 0:rank], preferred_element_type=jnp.float32)
            mixed = mixed * (1.0 / jnp.concatenate(totals, axis=0))
            att = mixed.astype(jnp.bfloat16)
            for h in range(group):
                at = pl.multiple_of((i * group + h) * tok + g * sub_tok, sub_tok)
                att_ref[pl.ds(at, sub_tok), :] = att[h * sub_tok : (h + 1) * sub_tok]

        def one_group(i, carry):
            for g in range(SUBS):
                if g + 1 < SUBS:
                    score(i, g + 1)
                else:
                    score(jnp.minimum(i + 1, n_groups - 1), 0)
                mix(i, g, soften(g))
            return carry

        score(0, 0)
        lax.fori_loop(0, n_groups, one_group, 0)

    block_start, end = jnp.int32(0), jnp.int32(0)
    for d in range(n_docs):
        end = end + lengths[d]
        block_start = jnp.where(seq * tok >= end, end, block_start)
    low = block_start - ((seq + 1) * tok - win)
    for tiles_out in range(LIGHT_TILES + 1):
        least = low >= tiles_out * KEY_TILE
        most = low < (tiles_out + 1) * KEY_TILE
        if tiles_out == 0:
            taken = most
        elif tiles_out == LIGHT_TILES:
            taken = least
        else:
            taken = least & most

        @pl.when(taken)
        def _(skip=tiles_out * KEY_TILE):
            groups_from(skip)

    wuv_copy.wait()
    n_outs = sem.shape[0] - 1
    outs = []
    heads_out = n_groups * group // n_outs
    for n in range(n_outs):
        for h in range(n * heads_out, (n + 1) * heads_out):
            o_ref[:, h * vdim : (h + 1) * vdim] = jnp.dot(
                att_ref[h * tok : (h + 1) * tok, :], wuv_ref[h], preferred_element_type=jnp.float32
            ).astype(o_ref.dtype)
        part = pl.ds(n * heads_out * vdim, heads_out * vdim)
        outs.append(pltpu.make_async_copy(o_ref.at[:, part], o_hbm.at[:, part], sem.at[1 + n]))
        outs[-1].start()
    for out in outs:
        out.wait()


def near(arrays):
    return [pltpu.with_memory_space_constraint(x, pltpu.VMEM) for x in arrays]


def far(arrays):
    return [pltpu.with_memory_space_constraint(x, pltpu.HBM) for x in arrays]


def per_device(queries, latent, w_uk, w_uv, doc_lengths):
    heads_dev, nope, rank = w_uk.shape
    vdim = w_uv.shape[2]
    tok = queries.shape[0]
    width = queries.shape[1] // heads_dev
    rows_per, lat = latent.shape
    n_seq, n_heads = lax.axis_size("seq"), lax.axis_size("heads")
    span = DOC_MOST // tok
    group = min(HEADS_GROUP, heads_dev)
    step = min(HEADS_STEP, heads_dev)
    rows = group * tok // SUBS
    kpad = -(-lat // LANES) * LANES

    edge = TAIL_MOST if n_seq == 2 * span else 0
    win = DOC_MOST + (edge or tok)
    hbm = pl.BlockSpec(memory_space=pl.ANY)
    vmem = pl.BlockSpec(memory_space=pltpu.VMEM)
    joined_type = pltpu.VMEM((heads_dev // group, SUBS, rows, kpad), jnp.bfloat16)
    steps = heads_dev // step

    def absorb_call(part, joined):
        base = steps * sum(PARTS[:part]) // sum(PARTS)
        count = steps * sum(PARTS[: part + 1]) // sum(PARTS) - base
        heads = count * step
        return pl.pallas_call(
            functools.partial(absorb, tok, nope, width, rank, lat, base),
            grid=(count,),
            in_specs=[
                pl.BlockSpec((tok, step * width), lambda i: (0, base + i)),
                pl.BlockSpec((step, nope, rank), lambda i: (base + i, 0, 0)),
            ]
            + [vmem] * (joined is not None),
            out_specs=vmem,
            out_shape=joined_type,
            compiler_params=pltpu.CompilerParams(vmem_limit_bytes=24 * 1024 * 1024),
            cost_estimate=pl.CostEstimate(
                flops=2 * tok * heads * nope * rank, bytes_accessed=4 * heads * nope * rank, transcendentals=0
            ),
            input_output_aliases={} if joined is None else {2: 0},
        )(*far([queries, w_uk]), *([] if joined is None else near([joined])))

    def swap(x, turn):
        return lax.ppermute(x, "heads", [(c, (c + turn) % n_heads) for c in range(n_heads)])

    bits = [latent] + [swap(latent, turn) for turn in range(1, n_heads)]
    if edge:
        source = span * n_heads - 1
        target = (span + span // 2 - 1) * n_heads
        bits += [lax.ppermute(latent, ("seq", "heads"), [(source, target + c)]) for c in range(n_heads)]
    joined = absorb_call(0, None)
    *bits, joined = lax.optimization_barrier((*bits, joined))
    own = pl.pallas_call(
        functools.partial(pack, n_heads, edge),
        in_specs=[vmem] * len(bits),
        out_specs=vmem,
        out_shape=pltpu.VMEM((tok + edge, lat), latent.dtype),
        compiler_params=pltpu.CompilerParams(vmem_limit_bytes=2 * 1024 * 1024),
    )(*near(bits))
    direct = []
    if edge:
        for ks in partners(span, n_heads):
            pairs = [
                (t * n_heads + c, (t ^ k) * n_heads + c) for c, k in enumerate(ks) if k for t in range(n_seq)
            ]
            direct.append(lax.ppermute(own, ("seq", "heads"), pairs))
    else:
        per = -(-span // n_heads)
        for n in range(per):
            pairs = []
            for c in range(n_heads):
                shift = 1 + c * per + n
                if shift <= span:
                    pairs += [(t * n_heads + c, (t + shift) * n_heads + c) for t in range(n_seq - shift)]
            direct.append(lax.ppermute(own, ("seq", "heads"), pairs))
    own, joined = lax.optimization_barrier((own, joined))
    joined = absorb_call(1, joined)
    for n in range(len(direct)):
        direct[n], joined = lax.optimization_barrier((direct[n], joined))
    pieces = list(direct)
    for turn in range(1, n_heads):
        pieces += [swap(x, turn) for x in direct]
    if len(PARTS) > 2:
        joined = absorb_call(2, joined)

    wpad = -(-win // KEY_TILE) * KEY_TILE
    plan = (
        n_heads, tok, rank, lat, vdim, win, wpad, span, doc_lengths.shape[0], width**-0.5 * math.log2(math.e),
        edge,
    )
    return pl.pallas_call(
        functools.partial(attend, plan),
        in_specs=[pl.BlockSpec(memory_space=pltpu.SMEM)] + [vmem] * (len(pieces) + 2) + [hbm],
        out_specs=hbm,
        out_shape=jax.ShapeDtypeStruct((tok, heads_dev * vdim), jnp.bfloat16),
        scratch_shapes=[
            pltpu.VMEM((win + tok, lat), jnp.bfloat16),
            pltpu.VMEM((kpad, wpad), jnp.bfloat16),
            pltpu.VMEM((tok, wpad), jnp.float32),
            pltpu.VMEM((rows, wpad), jnp.float32),
            pltpu.VMEM((rows, wpad), jnp.float32),
            pltpu.VMEM((rows, wpad), jnp.bfloat16),
            pltpu.VMEM((rows, wpad), jnp.bfloat16),
            pltpu.VMEM((heads_dev * tok, rank), jnp.bfloat16),
            pltpu.VMEM(w_uv.shape, w_uv.dtype),
            pltpu.VMEM((tok, heads_dev * vdim), jnp.bfloat16),
            pltpu.SemaphoreType.DMA((1 + OUT_PARTS,)),
        ],
        compiler_params=pltpu.CompilerParams(vmem_limit_bytes=40 * 1024 * 1024),
    )(doc_lengths, *near([own, *pieces, joined]), *far([w_uv]))


def solution(mesh):
    return jax.shard_map(
        per_device,
        mesh=mesh,
        in_specs=(
            P("seq", "heads"),
            P(("seq", "heads"), None),
            P("heads", None, None),
            P("heads", None, None),
            P(),
        ),
        out_specs=P("seq", "heads"),
        check_vma=False,
    )
```

```python
import functools
import math

import jax
import jax.numpy as jnp
from jax import lax
from jax.experimental import pallas as pl
from jax.experimental.pallas import tpu as pltpu
from jax.sharding import PartitionSpec as P

DOC_MOST = 1024
TAIL_MOST = 32
SUBS = 4
KEY_TILE = 256
LANES = 128
HEADS_GROUP = 8
HEADS_STEP = 8
PARTS = (1, 3)
LIGHT_TILES = 2
OUT_PARTS = 8
SOFT_ROWS = 16

far_negative = -1e30


def absorb(tok, nope, width, rank, lat, base, *refs):
    step = pl.program_id(0)
    q_ref, wuk_ref, j_ref = refs[0], refs[1], refs[-1]
    sub_tok = tok // SUBS
    rows = j_ref.shape[2]
    group = rows // sub_tok
    groups_step = wuk_ref.shape[0] // group
    kpad = j_ref.shape[3]

    for h in range(wuk_ref.shape[0]):
        absorbed = jnp.dot(
            q_ref[:, h * width : h * width + nope], wuk_ref[h], preferred_element_type=jnp.float32
        ).astype(jnp.bfloat16)
        rope = q_ref[:, h * width + nope : (h + 1) * width]
        if kpad > lat:
            rope = jnp.concatenate([rope, jnp.zeros((tok, kpad - lat), rope.dtype)], axis=1)
        i = (base + step) * groups_step + h // group
        at = (h % group) * sub_tok
        for g in range(SUBS):
            j_ref[i, g, at : at + sub_tok, 0:rank] = absorbed[g * sub_tok : (g + 1) * sub_tok]
            j_ref[i, g, at : at + sub_tok, rank:kpad] = rope[g * sub_tok : (g + 1) * sub_tok]


def pack(n_heads, edge, *refs):
    o_ref = refs[-1]
    core = lax.axis_index("heads")
    rows_per = refs[0].shape[0]
    for turn in range(n_heads):
        owner = lax.rem(core - turn + n_heads, n_heads)
        o_ref[pl.ds(pl.multiple_of(rows_per * owner, rows_per), rows_per), :] = refs[turn][...]
    if edge:
        rows = refs[n_heads][rows_per - edge :, :]
        for c in range(1, n_heads):
            rows = jnp.where(core == c, refs[n_heads + c][rows_per - edge :, :], rows)
        o_ref[rows_per * n_heads :, :] = rows


def partners(span, n_heads):
    ks = sorted(range(1, span), key=lambda k: (-k.bit_count(), k))
    per = -(-len(ks) // n_heads)
    ks += [0] * (per * n_heads - len(ks))
    return [ks[n * n_heads : (n + 1) * n_heads] for n in range(per)]


def attend(plan, lengths, *refs):
    (n_heads, tok, rank, lat, vdim, win, wpad, span, n_docs, factor, edge) = plan
    per = -(-(span - 1 if edge else span) // n_heads)
    own, refs = refs[0], refs[1:]
    pieces, refs = refs[: per * n_heads], refs[per * n_heads :]
    j_ref, wuv_hbm, o_hbm, win_ref, kt_ref, bias_ref, s0, s1, p0, p1, att_ref, wuv_ref, o_ref, sem = refs
    s_refs, p_refs = (s0, s1), (p0, p1)
    sub_tok = tok // SUBS
    n_groups, _, rows, kpad = j_ref.shape
    group = rows // sub_tok

    wuv_copy = pltpu.make_async_copy(wuv_hbm, wuv_ref, sem.at[0])
    wuv_copy.start()
    seq, core = lax.axis_index("seq"), lax.axis_index("heads")
    win_ref[win:, :] = jnp.zeros((win_ref.shape[0] - win, lat), win_ref.dtype)
    if edge:
        place = lax.rem(seq, span)
        held = [(own, place, place)]
        for turn in range(n_heads):
            owner = lax.rem(core - turn + n_heads, n_heads)
            for n, ks in enumerate(partners(span, n_heads)):
                k = jnp.int32(0)
                for c, kc in enumerate(ks):
                    k = jnp.where(owner == c, kc, k)
                block = lax.bitwise_xor(place, k)
                held.append((pieces[turn * per + n], block, jnp.where(k == 0, span, block)))
        for piece, block, _ in held[1:] + held[:1]:
            at = edge + tok * lax.rem(block - place - 1 + 2 * span, span)
            win_ref[pl.ds(pl.multiple_of(at, edge), tok), :] = piece[0:tok, :]
        win_ref[0:edge, :] = own[0:edge, :]
        for piece, _, block in held:
            at = jnp.where(block == span // 2 - 1, tok * (span - 1 - place), win)
            win_ref[pl.ds(pl.multiple_of(at, edge), edge), :] = piece[tok : tok + edge, :]
    else:
        win_ref[win - tok : win, :] = own[...]
        for turn in range(n_heads):
            owner = lax.rem(core - turn + n_heads, n_heads)
            for n in range(per):
                at = tok * (span - 1 - owner * per - n)
                win_ref[pl.ds(pl.multiple_of(at, tok), tok), :] = pieces[turn * per + n][...]
    q_pos = seq * tok + lax.broadcasted_iota(jnp.int32, (tok, LANES), 0)
    start = jnp.zeros((tok, LANES), jnp.int32)
    end = jnp.int32(0)
    for d in range(n_docs):
        end = end + lengths[d]
        start = jnp.where(q_pos >= end, end, start)
    for c in range(0, wpad, LANES):
        k_pos = (seq + 1) * tok - win + c + lax.broadcasted_iota(jnp.int32, (tok, LANES), 1)
        bias_ref[:, c : c + LANES] = jnp.where((k_pos >= start) & (k_pos <= q_pos), 0.0, far_negative)

    for r in range(0, wpad, LANES):
        n = min(LANES, max(win - r, 0))
        if n:
            kt_ref[0:lat, r : r + n] = win_ref[r : r + n, :].T
        if n < LANES:
            kt_ref[0:lat, r + n : r + LANES] = jnp.zeros((lat, LANES - n), kt_ref.dtype)
    if kpad > lat:
        kt_ref[lat:kpad, :] = jnp.zeros((kpad - lat, wpad), kt_ref.dtype)

    def groups_from(skip):
        def reach(g):
            return win - sub_tok * (SUBS - 1 - g)

        def tiles(g):
            n = -(-reach(g) // LANES) * LANES
            return [(c, min(KEY_TILE, n - c)) for c in range(skip, n, KEY_TILE)]

        def score(i, g):
            for c, w in tiles(g):
                s = jnp.dot(j_ref[i, g], kt_ref[:, c : c + w], preferred_element_type=jnp.float32)
                b = bias_ref[g * sub_tok : (g + 1) * sub_tok, c : c + w]
                s_refs[g % 2][:, c : c + w] = (s.reshape(group, sub_tok, w) + b[None]).reshape(rows, w)

        def soften(g):
            s_ref, p_ref = s_refs[g % 2], p_refs[g % 2]
            columns = [slice(cc, cc + LANES) for c, w in tiles(g) for cc in range(c, c + w, LANES)]
            totals = []
            for r in range(0, rows, SOFT_ROWS):
                s = [s_ref[r : r + SOFT_ROWS, at] for at in columns]
                top = jnp.max(functools.reduce(jnp.maximum, s), axis=1, keepdims=True)
                e = [jnp.exp2((x - top) * factor) for x in s]
                totals.append(jnp.sum(functools.reduce(jnp.add, e), axis=1, keepdims=True))
                for at, x in zip(columns, e):
                    p_ref[r : r + SOFT_ROWS, at] = x.astype(jnp.bfloat16)
            return totals

        def mix(i, g, totals):
            n = tiles(g)[-1][0] + tiles(g)[-1][1]
            mixed = jnp.dot(p_refs[g % 2][:, skip:n], win_ref[skip:n, 0:rank], preferred_element_type=jnp.float32)
            mixed = mixed * (1.0 / jnp.concatenate(totals, axis=0))
            att = mixed.astype(jnp.bfloat16)
            for h in range(group):
                at = pl.multiple_of((i * group + h) * tok + g * sub_tok, sub_tok)
                att_ref[pl.ds(at, sub_tok), :] = att[h * sub_tok : (h + 1) * sub_tok]

        def one_group(i, carry, last=False):
            for g in range(SUBS):
                if g + 1 < SUBS:
                    score(i, g + 1)
                elif not last:
                    score(i + 1, 0)
                mix(i, g, soften(g))
            return carry

        score(0, 0)
        lax.fori_loop(0, n_groups - 1, one_group, 0)
        one_group(n_groups - 1, 0, last=True)

    block_start, end = jnp.int32(0), jnp.int32(0)
    for d in range(n_docs):
        end = end + lengths[d]
        block_start = jnp.where(seq * tok >= end, end, block_start)
    low = block_start - ((seq + 1) * tok - win)
    for tiles_out in range(LIGHT_TILES + 1):
        least = low >= tiles_out * KEY_TILE
        most = low < (tiles_out + 1) * KEY_TILE
        if tiles_out == 0:
            taken = most
        elif tiles_out == LIGHT_TILES:
            taken = least
        else:
            taken = least & most

        @pl.when(taken)
        def _(skip=tiles_out * KEY_TILE):
            groups_from(skip)

    wuv_copy.wait()
    n_outs = sem.shape[0] - 1
    outs = []
    heads_out = n_groups * group // n_outs
    for n in range(n_outs):
        for h in range(n * heads_out, (n + 1) * heads_out):
            o_ref[:, h * vdim : (h + 1) * vdim] = jnp.dot(
                att_ref[h * tok : (h + 1) * tok, :], wuv_ref[h], preferred_element_type=jnp.float32
            ).astype(o_ref.dtype)
        part = pl.ds(n * heads_out * vdim, heads_out * vdim)
        outs.append(pltpu.make_async_copy(o_ref.at[:, part], o_hbm.at[:, part], sem.at[1 + n]))
        outs[-1].start()
    for out in outs:
        out.wait()


def near(arrays):
    return [pltpu.with_memory_space_constraint(x, pltpu.VMEM) for x in arrays]


def far(arrays):
    return [pltpu.with_memory_space_constraint(x, pltpu.HBM) for x in arrays]


def per_device(queries, latent, w_uk, w_uv, doc_lengths):
    heads_dev, nope, rank = w_uk.shape
    vdim = w_uv.shape[2]
    tok = queries.shape[0]
    width = queries.shape[1] // heads_dev
    rows_per, lat = latent.shape
    n_seq, n_heads = lax.axis_size("seq"), lax.axis_size("heads")
    span = DOC_MOST // tok
    group = min(HEADS_GROUP, heads_dev)
    step = min(HEADS_STEP, heads_dev)
    rows = group * tok // SUBS
    kpad = -(-lat // LANES) * LANES

    edge = TAIL_MOST if n_seq == 2 * span else 0
    win = DOC_MOST + (edge or tok)
    hbm = pl.BlockSpec(memory_space=pl.ANY)
    vmem = pl.BlockSpec(memory_space=pltpu.VMEM)
    joined_type = pltpu.VMEM((heads_dev // group, SUBS, rows, kpad), jnp.bfloat16)
    steps = heads_dev // step

    def absorb_call(part, joined):
        base = steps * sum(PARTS[:part]) // sum(PARTS)
        count = steps * sum(PARTS[: part + 1]) // sum(PARTS) - base
        heads = count * step
        return pl.pallas_call(
            functools.partial(absorb, tok, nope, width, rank, lat, base),
            grid=(count,),
            in_specs=[
                pl.BlockSpec((tok, step * width), lambda i: (0, base + i)),
                pl.BlockSpec((step, nope, rank), lambda i: (base + i, 0, 0)),
            ]
            + [vmem] * (joined is not None),
            out_specs=vmem,
            out_shape=joined_type,
            compiler_params=pltpu.CompilerParams(vmem_limit_bytes=24 * 1024 * 1024),
            cost_estimate=pl.CostEstimate(
                flops=2 * tok * heads * nope * rank, bytes_accessed=4 * heads * nope * rank, transcendentals=0
            ),
            input_output_aliases={} if joined is None else {2: 0},
        )(*far([queries, w_uk]), *([] if joined is None else near([joined])))

    def swap(x, turn):
        return lax.ppermute(x, "heads", [(c, (c + turn) % n_heads) for c in range(n_heads)])

    edges = []
    if edge:
        source = span * n_heads - 1
        target = (span + span // 2 - 1) * n_heads
        edges = [lax.ppermute(latent, ("seq", "heads"), [(source, target + c)]) for c in range(n_heads)]
    bits = [latent] + [swap(latent, turn) for turn in range(1, n_heads)] + edges
    joined = absorb_call(0, None)
    *bits, joined = lax.optimization_barrier((*bits, joined))
    own = pl.pallas_call(
        functools.partial(pack, n_heads, edge),
        in_specs=[vmem] * len(bits),
        out_specs=vmem,
        out_shape=pltpu.VMEM((tok + edge, lat), latent.dtype),
        compiler_params=pltpu.CompilerParams(vmem_limit_bytes=2 * 1024 * 1024),
    )(*near(bits))
    direct = []
    if edge:
        for ks in partners(span, n_heads):
            pairs = [
                (t * n_heads + c, (t ^ k) * n_heads + c) for c, k in enumerate(ks) if k for t in range(n_seq)
            ]
            direct.append(lax.ppermute(own, ("seq", "heads"), pairs))
    else:
        per = -(-span // n_heads)
        for n in range(per):
            pairs = []
            for c in range(n_heads):
                shift = 1 + c * per + n
                if shift <= span:
                    pairs += [(t * n_heads + c, (t + shift) * n_heads + c) for t in range(n_seq - shift)]
            direct.append(lax.ppermute(own, ("seq", "heads"), pairs))
    own, joined = lax.optimization_barrier((own, joined))
    joined = absorb_call(1, joined)
    for n in range(len(direct)):
        direct[n], joined = lax.optimization_barrier((direct[n], joined))
    pieces = list(direct)
    for turn in range(1, n_heads):
        pieces += [swap(x, turn) for x in direct]
    if len(PARTS) > 2:
        joined = absorb_call(2, joined)

    wpad = -(-win // KEY_TILE) * KEY_TILE
    plan = (
        n_heads, tok, rank, lat, vdim, win, wpad, span, doc_lengths.shape[0], width**-0.5 * math.log2(math.e),
        edge,
    )
    return pl.pallas_call(
        functools.partial(attend, plan),
        in_specs=[pl.BlockSpec(memory_space=pltpu.SMEM)] + [vmem] * (len(pieces) + 2) + [hbm],
        out_specs=hbm,
        out_shape=jax.ShapeDtypeStruct((tok, heads_dev * vdim), jnp.bfloat16),
        scratch_shapes=[
            pltpu.VMEM((win + tok, lat), jnp.bfloat16),
            pltpu.VMEM((kpad, wpad), jnp.bfloat16),
            pltpu.VMEM((tok, wpad), jnp.float32),
            pltpu.VMEM((rows, wpad), jnp.float32),
            pltpu.VMEM((rows, wpad), jnp.float32),
            pltpu.VMEM((rows, wpad), jnp.bfloat16),
            pltpu.VMEM((rows, wpad), jnp.bfloat16),
            pltpu.VMEM((heads_dev * tok, rank), jnp.bfloat16),
            pltpu.VMEM(w_uv.shape, w_uv.dtype),
            pltpu.VMEM((tok, heads_dev * vdim), jnp.bfloat16),
            pltpu.SemaphoreType.DMA((1 + OUT_PARTS,)),
        ],
        compiler_params=pltpu.CompilerParams(vmem_limit_bytes=40 * 1024 * 1024),
    )(doc_lengths, *near([own, *pieces, joined]), *far([w_uv]))


def solution(mesh):
    return jax.shard_map(
        per_device,
        mesh=mesh,
        in_specs=(
            P("seq", "heads"),
            P(("seq", "heads"), None),
            P("heads", None, None),
            P("heads", None, None),
            P(),
        ),
        out_specs=P("seq", "heads"),
        check_vma=False,
    )
```
